768 devices in a mesh: gx: 64 (over x, y, core), gy: 12 (over z).
Axes of the slice: x: 4, y: 8, z: 12, core: 2. Of those that a mesh axis runs over, the one named last changes fastest.
Arguments:
- block_input: bfloat16 [768, 40, 56, 256], P(('gx', 'gy')), may hold values from 0 to 6, as said below
- mid_first: bfloat16 [768, 40, 3584], P(('gx', 'gy')), may hold values from 0 to 6, as said below
- mid_second: bfloat16 [768, 40, 3584], P(('gx', 'gy')), may hold values from 0 to 18, as said below
- out_grad: bfloat16 [768, 40, 56, 256], P(('gx', 'gy')), may hold values from -6 to 6
- params: float32 [64, 1088], replicated, may hold values from -18 to 18
- velocity: float32 [64, 1088], P('gx'), may hold values from -1.8 to 1.8
Outputs:
- input_grad: bfloat16 [768, 40, 56, 256], P(('gx', 'gy'))
- new_velocity: float32 [64, 1088], P('gx')
- next_weights: float32 [64, 1088], replicated
The draws below stay inside these ranges and needn't reach their ends.
Inputs may be any that keep to these rules, and one draw needn't show every extreme that they name: `block_input`: ReLU outputs: nonnegative, about half of the entries zero. `mid_first`: ReLU outputs: nonnegative, about half of the entries zero. `mid_second`: ReLU outputs: nonnegative, about half of the entries zero.
All inputs are finite; a program needn't handle non-finite values.
Results may differ from the reference program's by a relative error of at most 0.0074.
Values sent between devices are 32-bit elements; how exact they have to be, the bound alone decides.
A program may use at most 64 MiB of HBM per device.

```python
import math
import jax
import jax.numpy as jnp
from jax import lax

C_IN = 256
C_MID = 64
H_DEV = 40
W_IMG = 56
K_ROW = 1088
STRIPS = 768


def relu_field(key, field_shape, channels, rising):
    key_base, key_scale = jax.random.split(key)
    base_draw = jax.random.truncated_normal(key_base, -4.0, 4.0, field_shape, jnp.float32)
    channel_scale = jnp.exp(jax.random.uniform(key_scale, (channels,), jnp.float32, math.log(0.5), math.log(1.5)))
    if rising:
        channel_scale = channel_scale * 3.0 ** (jnp.arange(channels, dtype=jnp.float32) / (channels - 1))
    return jnp.maximum(base_draw, 0.0) * channel_scale


def draw_block_input(key, part):
    field = relu_field(jax.random.fold_in(key, 11), (STRIPS, H_DEV, W_IMG, C_IN), C_IN, False)
    return field.astype(jnp.bfloat16)


def draw_mid_first(key, part):
    field = relu_field(jax.random.fold_in(key, 12), (STRIPS, H_DEV, W_IMG, C_MID), C_MID, False)
    return field.reshape(STRIPS, H_DEV, W_IMG * C_MID).astype(jnp.bfloat16)


def draw_mid_second(key, part):
    field = relu_field(jax.random.fold_in(key, 13), (STRIPS, H_DEV, W_IMG, C_MID), C_MID, True)
    return field.reshape(STRIPS, H_DEV, W_IMG * C_MID).astype(jnp.bfloat16)


def draw_params(key, part):
    key_base, key_scale = jax.random.split(jax.random.fold_in(key, 14))
    base_draw = jax.random.truncated_normal(key_base, -4.0, 4.0, (C_MID, K_ROW), jnp.float32)
    row_scale = jnp.exp(jax.random.uniform(key_scale, (C_MID,), jnp.float32, math.log(0.4), math.log(1.5)))
    row_scale = row_scale * 3.0 ** (jnp.arange(C_MID, dtype=jnp.float32) / (C_MID - 1))
    return base_draw * row_scale[:, None]


def block_levels(rng, extent, shards, low, high):
    level = 1.0
    for dim, blocks in shards:
        steps = jax.random.uniform(jax.random.fold_in(jax.random.fold_in(rng, 6), dim), (blocks,), jnp.float32, low / len(shards), high / len(shards))
        level = level * jnp.repeat(jnp.exp(steps), extent[dim] // blocks).reshape((-1,) + (1,) * (len(extent) - 1 - dim))
    return level


def scatter_about(own_key, extent, width, reach, cuts=(), kind=jnp.bfloat16):
    loudness = block_levels(own_key, extent, cuts, -0.22, 0.18) if cuts else 1.0
    values = jax.random.normal(own_key, extent, jnp.float32) * width * loudness
    return jnp.minimum(jnp.maximum(values, -reach), reach).astype(kind)


def setup_inputs(seed: int = 0) -> dict:
    seeds = jax.random.split(jax.random.key(seed), 7)
    block_input = draw_block_input(jax.random.fold_in(seeds[6], 71), 0)
    mid_first = draw_mid_first(jax.random.fold_in(seeds[6], 71), 0)
    mid_second = draw_mid_second(jax.random.fold_in(seeds[6], 71), 0)
    out_grad = scatter_about(seeds[3], (STRIPS, H_DEV, W_IMG, C_IN), 1.0, 6.0, ((0, 768),))
    params = draw_params(jax.random.fold_in(seeds[6], 71), 0)
    velocity = scatter_about(seeds[5], (C_MID, K_ROW), 0.3, 1.8, ((0, 64),), jnp.float32)
    return {"block_input": block_input, "mid_first": mid_first, "mid_second": mid_second, "out_grad": out_grad, "params": params, "velocity": velocity}


learn_rate = 0.5
momentum = 0.9
norm_eps = 1e-06

def tap_patches(field):
    img_height, img_width = (field.shape[0], field.shape[1])
    padded = jnp.pad(field, ((1, 1), (1, 1), (0, 0)))
    pieces = [padded[tap_row:tap_row + img_height, tap_col:tap_col + img_width] for tap_row in range(3) for tap_col in range(3)]
    return jnp.concatenate(pieces, axis=2).reshape(img_height * img_width, 9 * field.shape[2])

def tap_sum(spread):
    img_height, img_width = (spread.shape[0], spread.shape[1])
    padded = jnp.pad(spread, ((1, 1), (1, 1), (0, 0), (0, 0)))
    result = jnp.zeros((img_height, img_width, spread.shape[3]), jnp.float32)
    for tap_row in range(3):
        for tap_col in range(3):
            result = result + padded[2 - tap_row:2 - tap_row + img_height, 2 - tap_col:2 - tap_col + img_width, 3 * tap_row + tap_col]
    return result

def outer_sum(left, right):
    return lax.dot_general(left, right, (((0,), (0,)), ((), ())), preferred_element_type=jnp.float32)

def strip_backward(x_strip, first_strip, second_strip, grad_strip, weights):
    img_height, img_width = (x_strip.shape[0], x_strip.shape[1])
    pixels = img_height * img_width
    scale_one = 1.0 / math.sqrt(C_IN)
    scale_two = 1.0 / math.sqrt(9 * C_MID)
    scale_three = 1.0 / math.sqrt(C_MID)
    w_first = weights[:, :C_IN]
    w_second = weights[:, C_IN:C_IN + 9 * C_MID]
    w_third = weights[:, C_IN + 9 * C_MID:]
    input_flat = x_strip.reshape(pixels, C_IN)
    out_flat = grad_strip.reshape(pixels, C_IN)
    first_field = first_strip.reshape(img_height, img_width, C_MID)
    second_flat = second_strip.reshape(pixels, C_MID)
    back_second = lax.dot_general(out_flat, w_third, (((1,), (1,)), ((), ())), preferred_element_type=jnp.float32) * scale_three
    back_second = jnp.where(second_flat > 0, back_second, 0.0).astype(jnp.bfloat16)
    spread = jnp.dot(back_second, w_second, preferred_element_type=jnp.float32) * scale_two
    back_first = tap_sum(spread.reshape(img_height, img_width, 9, C_MID))
    back_first = jnp.where(first_field > 0, back_first, 0.0).astype(jnp.bfloat16).reshape(pixels, C_MID)
    input_grad = (out_flat.astype(jnp.float32) + scale_one * jnp.dot(back_first, w_first, preferred_element_type=jnp.float32)).astype(jnp.bfloat16)
    patches = tap_patches(first_field)
    term = jnp.concatenate([scale_one * outer_sum(back_first, input_flat), scale_two * outer_sum(back_second, patches), scale_three * outer_sum(second_flat, out_flat)], axis=1)
    return (input_grad.reshape(img_height, img_width, C_IN), term)

def layer_squares(matrix):
    return jnp.stack([jnp.sum(matrix[:, :C_IN] ** 2), jnp.sum(matrix[:, C_IN:C_IN + 9 * C_MID] ** 2), jnp.sum(matrix[:, C_IN + 9 * C_MID:] ** 2)])

def trust_columns(trust_ratio):
    return jnp.concatenate([jnp.broadcast_to(trust_ratio[0], (C_IN,)), jnp.broadcast_to(trust_ratio[1], (9 * C_MID,)), jnp.broadcast_to(trust_ratio[2], (C_IN,))])

def reference(block_input, mid_first, mid_second, out_grad, params, velocity):
    weights = params.astype(jnp.bfloat16)

    def step(grad_total, strip_items):
        input_grad, term = strip_backward(strip_items[0], strip_items[1], strip_items[2], strip_items[3], weights)
        return (grad_total + term, input_grad)
    grad_total, input_grads = lax.scan(step, jnp.zeros((C_MID, K_ROW), jnp.float32), (block_input, mid_first, mid_second, out_grad))
    grad_mean = grad_total / STRIPS
    trust_ratio = jnp.sqrt(layer_squares(params)) / (jnp.sqrt(layer_squares(grad_mean)) + norm_eps)
    new_velocity = momentum * velocity + learn_rate * trust_columns(trust_ratio)[None, :] * grad_mean
    next_weights = params - new_velocity
    return (input_grads, new_velocity, next_weights)
```

```python
import functools
import math

import jax
import jax.numpy as jnp
from jax import lax
from jax.experimental import pallas as pl
from jax.experimental.pallas import tpu as pltpu
from jax.sharding import PartitionSpec as P

C_IN = 256
C_MID = 64
H_DEV = 40
W_IMG = 56
W_PAD = 64
K_ROW = 1088
K_PAD = 1152
PIXELS = H_DEV * W_PAD
ROWS_X = 4
ROWS_Y = 8
CORES = 2

H_CHUNK = 4
CHUNK = H_CHUNK * W_PAD
CHUNKS = H_DEV // H_CHUNK

learn_rate = 0.5
momentum = 0.9
norm_eps = 1e-06

F32 = jnp.float32
BF16 = jnp.bfloat16
MESH = pl.DeviceIdType.MESH

PART_W1 = (0, 256)
PART_W3 = (256, 256)
PART_W2 = (512, 640)


def dot(left, right, left_dim, right_dim):
    return lax.dot_general(
        left, right, (((left_dim,), (right_dim,)), ((), ())), preferred_element_type=F32
    )


def spread_pixels(fields, out):
    low = lax.broadcasted_iota(jnp.int32, (H_DEV, 128), 1) < 64
    for pair in range(W_IMG // 2):
        both = fields[:, 128 * pair : 128 * (pair + 1)].astype(F32)
        swapped = pltpu.roll(both, 64, 1)
        out[pl.ds(2 * pair, H_DEV, stride=W_PAD), :] = jnp.where(low, both, swapped)
        out[pl.ds(2 * pair + 1, H_DEV, stride=W_PAD), :] = jnp.where(low, swapped, both)
    zeros = jnp.zeros((W_PAD - W_IMG, 128), F32)
    for row in range(H_DEV):
        out[row * W_PAD + W_IMG : (row + 1) * W_PAD, :] = zeros


def padded_chunk(ref, chunk):
    values = ref[pl.ds(chunk * H_CHUNK, H_CHUNK)].astype(F32)
    zeros = jnp.zeros((H_CHUNK, W_PAD - W_IMG, C_IN), F32)
    return jnp.concatenate([values, zeros], axis=1).reshape(CHUNK, C_IN).astype(BF16)


def total(values):
    return jnp.sum(jnp.sum(values * values, axis=0, keepdims=True), axis=1, keepdims=True)


def kernel(
    size_x,
    size_y,
    size_z,
    x_hbm,
    first_hbm,
    second_hbm,
    grad_hbm,
    params,
    velocity,
    input_grad_hbm,
    new_velocity,
    next_weights,
    x_vmem,
    first_vmem,
    second_vmem,
    grad_vmem,
    input_grad_vmem,
    first_pix,
    second_pix,
    taps,
    back_first,
    w_first,
    w_second,
    w_third,
    sum_one,
    sum_two,
    sum_three,
    local,
    got_one,
    rows_two,
    got_two,
    got_three,
    rows_four,
    grads,
    velocities,
    velocity_flat,
    load_sem,
    store_sem,
    send_one,
    recv_one,
    send_two,
    recv_two,
    send_three,
    recv_three,
    send_four,
    recv_four,
    send_five,
    recv_five,
    send_vel,
    recv_vel,
):
    groups = size_x * CORES
    group_rows = C_MID // groups
    own_rows = group_rows // size_y
    strips = groups * size_y * size_z
    scale_one = 1.0 / math.sqrt(C_IN)
    scale_two = 1.0 / math.sqrt(9 * C_MID)
    scale_three = 1.0 / math.sqrt(C_MID)
    mean_factor = 1.0 / strips

    gx = lax.axis_index("gx")
    my_z = lax.axis_index("gy")
    my_core = lax.rem(gx, CORES)
    my_y = lax.rem(gx // CORES, size_y)
    my_x = gx // (CORES * size_y)
    my_group = my_x * CORES + my_core

    def group_peer(step):
        peer = lax.rem(my_group + step, groups)
        index = ((peer // CORES) * size_y + my_y) * CORES + lax.rem(peer, CORES)
        return peer, (index, my_z)

    def y_peer(step):
        peer = lax.rem(my_y + step, size_y)
        return peer, ((my_x * size_y + peer) * CORES + my_core, my_z)

    def z_peer(step):
        peer = lax.rem(my_z + step, size_z)
        return peer, (gx, peer)

    axes = ((groups, group_peer), (size_y, y_peer), (size_z, z_peer))

    loads = []
    for index, (src, dst) in enumerate(
        (
            (second_hbm, second_vmem),
            (grad_hbm, grad_vmem),
            (first_hbm, first_vmem),
            (x_hbm, x_vmem),
        )
    ):
        load = pltpu.make_async_copy(src.at[0], dst, load_sem.at[index])
        load.start()
        loads.append(load)

    barrier = pltpu.get_barrier_semaphore()
    for size, peer_of in axes:
        for step in range(1, size):
            pl.semaphore_signal(barrier, inc=1, device_id=peer_of(step)[1], device_id_type=MESH)

    weights = params[...].astype(BF16)
    w_first[...] = weights[:, :C_IN]
    for tap_row in range(3):
        start = C_IN + 3 * C_MID * tap_row
        w_second[C_MID * tap_row : C_MID * (tap_row + 1), :] = weights[:, start : start + 3 * C_MID]
        w_third[C_MID * tap_row : C_MID * (tap_row + 1), :] = weights[:, C_IN + 9 * C_MID :]

    sum_one[...] = jnp.zeros_like(sum_one)
    sum_two[...] = jnp.zeros_like(sum_two)
    sum_three[...] = jnp.zeros_like(sum_three)
    no_taps = jnp.zeros((W_PAD, C_MID), BF16)
    taps[W_PAD : 2 * W_PAD, 2 * C_MID :] = no_taps
    taps[PIXELS : PIXELS + W_PAD, :C_MID] = no_taps

    loads[0].wait()
    spread_pixels(second_vmem, second_pix)
    loads[1].wait()

    def step_second(chunk, carry):
        start = pl.multiple_of(chunk * CHUNK, CHUNK)
        out_grad = padded_chunk(grad_vmem, chunk)
        second = second_pix[pl.ds(start, CHUNK), :]
        back = dot(out_grad, w_third[...], 1, 1) * scale_three
        both = jnp.where(second > 0, back[:, :128], 0.0).astype(BF16)
        last = jnp.where(second[:, :C_MID] > 0, back[:, 128:], 0.0).astype(BF16)
        taps[pl.ds(start, CHUNK), :C_MID] = both[:, :C_MID]
        taps[pl.ds(start + W_PAD, CHUNK), C_MID : 2 * C_MID] = both[:, C_MID:]
        taps[pl.ds(start + 2 * W_PAD, CHUNK), 2 * C_MID :] = last
        sum_three[...] += dot(second[:, :C_MID].astype(BF16), out_grad, 0, 0)
        return carry

    lax.fori_loop(0, CHUNKS, step_second, 0)

    def place(columns, values):
        local[:, :, columns : columns + values.shape[1]] = values.reshape(
            groups, group_rows, values.shape[1]
        )

    def part_copy(index, columns, peer, slot, device):
        return pltpu.make_async_remote_copy(
            src_ref=local.at[peer, :, pl.ds(*columns)],
            dst_ref=got_one.at[slot, :, pl.ds(*columns)],
            send_sem=send_one.at[index, peer],
            recv_sem=recv_one.at[index, slot],
            device_id=device,
            device_id_type=MESH,
        )

    parts = (PART_W3, PART_W2, PART_W1)

    def send_part(index):
        for step in range(1, groups):
            peer, device = group_peer(step)
            part_copy(index, parts[index], peer, my_group, device).start()

    def velocity_copy(kind, ref, slot, device):
        return pltpu.make_async_remote_copy(
            src_ref=ref,
            dst_ref=ref,
            send_sem=send_vel.at[kind, slot[0]],
            recv_sem=recv_vel.at[kind, slot[1]],
            device_id=device,
            device_id_type=MESH,
        )

    place(PART_W3[0], sum_three[...] * (scale_three * mean_factor))
    velocities[my_x, my_y, my_core] = velocity[...]
    pl.semaphore_wait(barrier, sum(size - 1 for size, _ in axes))
    send_part(0)
    for step in range(1, size_y):
        peer, device = y_peer(step)
        velocity_copy(0, velocities.at[my_x, my_y, my_core], (peer, my_y), device).start()

    loads[2].wait()
    spread_pixels(first_vmem, first_pix)
    loads[3].wait()

    low = lax.broadcasted_iota(jnp.int32, (CHUNK, 128), 1) < 64

    def step_first(chunk, carry):
        start = pl.multiple_of(chunk * CHUNK, CHUNK)
        first = first_pix[pl.ds(start, CHUNK), :]
        tap = taps[pl.ds(start + W_PAD, CHUNK), :]
        shifted = jnp.concatenate(
            [
                jnp.where(low, pltpu.roll(first, 1, 0), first),
                pltpu.roll(first, CHUNK - 1, 0)[:, :C_MID],
            ],
            axis=1,
        ).astype(BF16)
        sum_two[...] += dot(tap, shifted, 0, 0)
        spread = dot(tap, w_second[...], 1, 0)
        mixed = (
            pltpu.roll(spread[:, :128], CHUNK - 1, 0)[:, :C_MID]
            + spread[:, C_MID : 2 * C_MID]
            + pltpu.roll(spread[:, 128:], 1, 0)
        ) * scale_two
        back = jnp.where(first[:, :C_MID] > 0, mixed, 0.0).astype(BF16)
        back_first[pl.ds(start, CHUNK), :] = back
        sum_one[...] += dot(back, padded_chunk(x_vmem, chunk), 0, 0)
        return carry

    lax.fori_loop(0, CHUNKS, step_first, 0)

    for tap_row in range(3):
        place(
            PART_W2[0] + 3 * C_MID * tap_row,
            sum_two[C_MID * tap_row : C_MID * (tap_row + 1), :] * (scale_two * mean_factor),
        )
    local[:, :, K_ROW:] = jnp.zeros((groups, group_rows, K_PAD - K_ROW), F32)
    place(PART_W1[0], sum_one[...] * (scale_one * mean_factor))
    send_part(1)
    send_part(2)

    for step in range(1, size_y):
        peer, device = y_peer(step)
        velocity_copy(0, velocities.at[my_x, peer, my_core], (peer, peer), device).wait_recv()
    for step in range(1, groups):
        peer, device = group_peer(step)
        velocity_copy(1, velocities.at[my_x, :, my_core], (peer, my_group), device).start()

    def step_input(chunk, carry):
        start = pl.multiple_of(chunk * CHUNK, CHUNK)
        rise = dot(back_first[pl.ds(start, CHUNK), :], w_first[...], 1, 0) * scale_one
        rise = rise.reshape(H_CHUNK, W_PAD, C_IN)[:, :W_IMG]
        rows = pl.ds(chunk * H_CHUNK, H_CHUNK)
        input_grad_vmem[rows] = (grad_vmem[rows].astype(F32) + rise).astype(BF16)
        return carry

    lax.fori_loop(0, CHUNKS, step_input, 0)
    store = pltpu.make_async_copy(input_grad_vmem, input_grad_hbm.at[0], store_sem)
    store.start()

    block = local[my_group]
    for step in range(1, groups):
        peer, device = group_peer(step)
        for index in range(3):
            part_copy(index, parts[index], peer, peer, device).wait_recv()
        block = block + got_one[peer]
    for index in range(size_y):
        rows_two[index] = block[index * own_rows : (index + 1) * own_rows]

    def two_copy(peer, slot, device):
        return pltpu.make_async_remote_copy(
            src_ref=rows_two.at[peer],
            dst_ref=got_two.at[slot],
            send_sem=send_two.at[peer],
            recv_sem=recv_two.at[slot],
            device_id=device,
            device_id_type=MESH,
        )

    for step in range(1, size_y):
        peer, device = y_peer(step)
        two_copy(peer, my_y, device).start()
    row = rows_two[my_y]
    for step in range(1, size_y):
        peer, device = y_peer(step)
        two_copy(peer, peer, device).wait_recv()
        row = row + got_two[peer]

    def three_copy(slot, peer, device):
        return pltpu.make_async_remote_copy(
            src_ref=got_three.at[slot],
            dst_ref=got_three.at[slot],
            send_sem=send_three.at[peer],
            recv_sem=recv_three.at[slot],
            device_id=device,
            device_id_type=MESH,
        )

    got_three[my_z] = row
    for step in range(1, size_z):
        peer, device = z_peer(step)
        three_copy(my_z, peer, device).start()
    for step in range(1, size_z):
        peer, device = z_peer(step)
        three_copy(peer, peer, device).wait_recv()
    row = got_three[0]
    for index in range(1, size_z):
        row = row + got_three[index]

    def four_copy(slot, peer, device):
        return pltpu.make_async_remote_copy(
            src_ref=rows_four.at[slot],
            dst_ref=rows_four.at[slot],
            send_sem=send_four.at[peer],
            recv_sem=recv_four.at[slot],
            device_id=device,
            device_id_type=MESH,
        )

    rows_four[my_y] = row
    for step in range(1, size_y):
        peer, device = y_peer(step)
        four_copy(my_y, peer, device).start()

    for step in range(1, groups):
        peer, device = group_peer(step)
        other = velocities.at[peer // CORES, :, lax.rem(peer, CORES)]
        velocity_copy(1, other, (peer, peer), device).wait_recv()
    for at_x in range(size_x):
        for at_y in range(size_y):
            for at_core in range(CORES):
                index = (at_x * size_y + at_y) * CORES + at_core
                velocity_flat[index * own_rows : (index + 1) * own_rows, :] = velocities[
                    at_x, at_y, at_core
                ]
    bounds = (
        (0, C_IN, PART_W1[0]),
        (C_IN, C_IN + 9 * C_MID, PART_W2[0]),
        (C_IN + 9 * C_MID, K_ROW, PART_W3[0]),
    )
    weight_norms = [jnp.sqrt(total(params[:, low_end:high_end])) for low_end, high_end, _ in bounds]

    for step in range(1, size_y):
        peer, device = y_peer(step)
        four_copy(peer, peer, device).wait_recv()
    for index in range(size_y):
        grads[my_group, index * own_rows : (index + 1) * own_rows, :] = rows_four[index]

    def five_copy(slot, peer, device):
        return pltpu.make_async_remote_copy(
            src_ref=grads.at[slot],
            dst_ref=grads.at[slot],
            send_sem=send_five.at[peer],
            recv_sem=recv_five.at[slot],
            device_id=device,
            device_id_type=MESH,
        )

    for step in range(1, groups):
        peer, device = group_peer(step)
        five_copy(my_group, peer, device).start()
    for step in range(1, groups):
        peer, device = group_peer(step)
        five_copy(peer, peer, device).wait_recv()

    for (low_end, high_end, column), weight_norm in zip(bounds, weight_norms):
        grad = grads[:, :, column : column + high_end - low_end].reshape(
            C_MID, high_end - low_end
        )
        rate = learn_rate * (weight_norm / (jnp.sqrt(total(grad)) + norm_eps))
        fresh = momentum * velocity_flat[:, low_end:high_end] + rate * grad
        velocity_flat[:, low_end:high_end] = fresh
        next_weights[:, low_end:high_end] = params[:, low_end:high_end] - fresh
    new_velocity[...] = velocity_flat[pl.ds(gx * own_rows, own_rows), :]

    for step in range(1, groups):
        peer, device = group_peer(step)
        for index in range(3):
            part_copy(index, parts[index], peer, my_group, device).wait_send()
        velocity_copy(1, velocities.at[my_x, :, my_core], (peer, my_group), device).wait_send()
        five_copy(my_group, peer, device).wait_send()
    for step in range(1, size_y):
        peer, device = y_peer(step)
        velocity_copy(0, velocities.at[my_x, my_y, my_core], (peer, my_y), device).wait_send()
        two_copy(peer, my_y, device).wait_send()
        four_copy(my_y, peer, device).wait_send()
    for step in range(1, size_z):
        peer, device = z_peer(step)
        three_copy(my_z, peer, device).wait_send()
    store.wait()


def shards(size_x, size_y, size_z, block_input, mid_first, mid_second, out_grad, params, velocity):
    groups = size_x * CORES
    group_rows = C_MID // groups
    own_rows = group_rows // size_y
    dma = pltpu.SemaphoreType.DMA
    return pl.pallas_call(
        functools.partial(kernel, size_x, size_y, size_z),
        out_shape=(
            jax.ShapeDtypeStruct((1, H_DEV, W_IMG, C_IN), BF16),
            jax.ShapeDtypeStruct((own_rows, K_ROW), F32),
            jax.ShapeDtypeStruct((C_MID, K_ROW), F32),
        ),
        in_specs=[pl.BlockSpec(memory_space=pl.ANY)] * 4
        + [pl.BlockSpec(memory_space=pltpu.VMEM)] * 2,
        out_specs=(
            pl.BlockSpec(memory_space=pl.ANY),
            pl.BlockSpec(memory_space=pltpu.VMEM),
            pl.BlockSpec(memory_space=pltpu.VMEM),
        ),
        scratch_shapes=[
            pltpu.VMEM((H_DEV, W_IMG, C_IN), BF16),
            pltpu.VMEM((H_DEV, W_IMG * C_MID), BF16),
            pltpu.VMEM((H_DEV, W_IMG * C_MID), BF16),
            pltpu.VMEM((H_DEV, W_IMG, C_IN), BF16),
            pltpu.VMEM((H_DEV, W_IMG, C_IN), BF16),
            pltpu.VMEM((PIXELS, 128), F32),
            pltpu.VMEM((PIXELS, 128), F32),
            pltpu.VMEM((PIXELS + 2 * W_PAD, 3 * C_MID), BF16),
            pltpu.VMEM((PIXELS, C_MID), BF16),
            pltpu.VMEM((C_MID, C_IN), BF16),
            pltpu.VMEM((3 * C_MID, 3 * C_MID), BF16),
            pltpu.VMEM((3 * C_MID, C_IN), BF16),
            pltpu.VMEM((C_MID, C_IN), F32),
            pltpu.VMEM((3 * C_MID, 3 * C_MID), F32),
            pltpu.VMEM((C_MID, C_IN), F32),
            pltpu.VMEM((groups, group_rows, K_PAD), F32),
            pltpu.VMEM((groups, group_rows, K_PAD), F32),
            pltpu.VMEM((size_y, own_rows, K_PAD), F32),
            pltpu.VMEM((size_y, own_rows, K_PAD), F32),
            pltpu.VMEM((size_z, own_rows, K_PAD), F32),
            pltpu.VMEM((size_y, own_rows, K_PAD), F32),
            pltpu.VMEM((groups, group_rows, K_PAD), F32),
            pltpu.VMEM((size_x, size_y, CORES, own_rows, K_ROW), F32),
            pltpu.VMEM((C_MID, K_ROW), F32),
            dma((4,)),
            dma,
            dma((3, groups)),
            dma((3, groups)),
            dma((size_y,)),
            dma((size_y,)),
            dma((size_z,)),
            dma((size_z,)),
            dma((size_y,)),
            dma((size_y,)),
            dma((groups,)),
            dma((groups,)),
            dma((2, max(groups, size_y))),
            dma((2, max(groups, size_y))),
        ],
        compiler_params=pltpu.CompilerParams(
            collective_id=0, has_side_effects=True, vmem_limit_bytes=62 * 1024 * 1024
        ),
        name="bottleneck_backward",
    )(block_input, mid_first, mid_second, out_grad, params, velocity)


def solution(mesh):
    return jax.shard_map(
        functools.partial(shards, ROWS_X, ROWS_Y, mesh.shape["gy"]),
        mesh=mesh,
        in_specs=(
            P(("gx", "gy"), None, None, None),
            P(("gx", "gy"), None, None),
            P(("gx", "gy"), None, None),
            P(("gx", "gy"), None, None, None),
            P(),
            P("gx", None),
        ),
        out_specs=(P(("gx", "gy"), None, None, None), P("gx", None), P()),
        check_vma=False,
    )
```

```python
import functools
import math

import jax
import jax.numpy as jnp
from jax import lax
from jax.experimental import pallas as pl
from jax.experimental.pallas import tpu as pltpu
from jax.sharding import PartitionSpec as P

C_IN = 256
C_MID = 64
H_DEV = 40
W_IMG = 56
W_PAD = 64
K_ROW = 1088
K_PAD = 1152
PIXELS = H_DEV * W_PAD
ROWS_X = 4
ROWS_Y = 8
CORES = 2

H_CHUNK = 8
CHUNK = H_CHUNK * W_PAD
CHUNKS = H_DEV // H_CHUNK

learn_rate = 0.5
momentum = 0.9
norm_eps = 1e-06

F32 = jnp.float32
BF16 = jnp.bfloat16
MESH = pl.DeviceIdType.MESH

AT_W3 = 0
AT_W1 = 256
AT_W2 = 512
PARTS = ((0, K_PAD),)


def dot(left, right, left_dim, right_dim):
    return lax.dot_general(
        left, right, (((left_dim,), (right_dim,)), ((), ())), preferred_element_type=F32
    )


def spread_pixels(fields, out):
    low = lax.broadcasted_iota(jnp.int32, (H_DEV, 128), 1) < 64
    for pair in range(W_IMG // 2):
        both = fields[:, 128 * pair : 128 * (pair + 1)].astype(F32)
        swapped = pltpu.roll(both, 64, 1)
        out[pl.ds(2 * pair, H_DEV, stride=W_PAD), :] = jnp.where(low, both, swapped)
        out[pl.ds(2 * pair + 1, H_DEV, stride=W_PAD), :] = jnp.where(low, swapped, both)
    zeros = jnp.zeros((W_PAD - W_IMG, 128), F32)
    for row in range(H_DEV):
        out[row * W_PAD + W_IMG : (row + 1) * W_PAD, :] = zeros


def padded_chunk(ref, chunk):
    values = ref[chunk * H_CHUNK : (chunk + 1) * H_CHUNK].astype(F32)
    zeros = jnp.zeros((H_CHUNK, W_PAD - W_IMG, C_IN), F32)
    return jnp.concatenate([values, zeros], axis=1).reshape(CHUNK, C_IN).astype(BF16)


def each_chunk(step):
    for chunk in range(CHUNKS):
        step(chunk)


def total(values):
    return jnp.sum(jnp.sum(values * values, axis=0, keepdims=True), axis=1, keepdims=True)


def kernel(
    size_x,
    size_y,
    size_z,
    x_hbm,
    first_hbm,
    second_hbm,
    grad_hbm,
    params_hbm,
    velocity_hbm,
    input_grad,
    new_velocity,
    next_weights,
    x_vmem,
    first_vmem,
    second_vmem,
    grad_vmem,
    params,
    velocity,
    first_pix,
    second_pix,
    taps,
    back_first,
    w_first,
    w_second,
    w_third,
    sum_one,
    sum_two,
    sum_three,
    local,
    got_one,
    rows_two,
    got_two,
    got_three,
    rows_four,
    grads,
    velocities,
    velocity_flat,
    load_sem,
    send_one,
    recv_one,
    send_two,
    recv_two,
    send_three,
    recv_three,
    send_four,
    recv_four,
    send_five,
    recv_five,
    send_vel,
    recv_vel,
):
    groups = size_x * CORES
    group_rows = C_MID // groups
    own_rows = group_rows // size_y
    strips = groups * size_y * size_z
    scale_one = 1.0 / math.sqrt(C_IN)
    scale_two = 1.0 / math.sqrt(9 * C_MID)
    scale_three = 1.0 / math.sqrt(C_MID)
    mean_factor = 1.0 / strips

    def rows_of(chunk):
        return pl.ds(chunk * H_CHUNK, H_CHUNK)

    def load(src, dst, slot):
        copy = pltpu.make_async_copy(src, dst, load_sem.at[slot])
        copy.start()
        return copy

    load_params = load(params_hbm, params, 0)
    load_second = load(second_hbm.at[0], second_vmem, 1)
    load_grad = load(grad_hbm.at[0], grad_vmem, 2)
    load_first = load(first_hbm.at[0], first_vmem, 3)
    load_x = load(x_hbm.at[0], x_vmem, 4)
    load_velocity = load(velocity_hbm, velocity, 5)

    gx = lax.axis_index("gx")
    my_z = lax.axis_index("gy")
    my_core = lax.rem(gx, CORES)
    my_y = lax.rem(gx // CORES, size_y)
    my_x = gx // (CORES * size_y)
    my_group = my_x * CORES + my_core

    def wrap(index, size):
        return jnp.where(index >= size, index - size, index)

    group_peers = []
    for step in range(size_x):
        peer_x = wrap(my_x + step, size_x)
        for core in (my_core, 1 - my_core) if step else (1 - my_core,):
            index = (peer_x * size_y + my_y) * CORES + core
            group_peers.append((peer_x * CORES + core, (index, my_z), peer_x, core))
    y_peers = []
    for step in range(1, size_y):
        peer = wrap(my_y + step, size_y)
        y_peers.append((peer, ((my_x * size_y + peer) * CORES + my_core, my_z)))
    z_peers = []
    for step in range(1, size_z):
        peer = wrap(my_z + step, size_z)
        z_peers.append((peer, (gx, peer)))

    barrier = pltpu.get_barrier_semaphore()
    everyone = [peer[1] for peer in group_peers + y_peers + z_peers]
    for device in everyone:
        pl.semaphore_signal(barrier, inc=1, device_id=device, device_id_type=MESH)

    load_params.wait()
    weights = params[...].astype(BF16)
    w_first[...] = weights[:, :C_IN]
    for tap_row in range(3):
        start = C_IN + 3 * C_MID * tap_row
        w_second[C_MID * tap_row : C_MID * (tap_row + 1), :] = weights[:, start : start + 3 * C_MID]
        w_third[C_MID * tap_row : C_MID * (tap_row + 1), :] = weights[:, C_IN + 9 * C_MID :]

    sum_one[...] = jnp.zeros_like(sum_one)
    sum_two[...] = jnp.zeros_like(sum_two)
    sum_three[...] = jnp.zeros_like(sum_three)
    no_taps = jnp.zeros((W_PAD, C_MID), BF16)
    taps[W_PAD : 2 * W_PAD, 2 * C_MID :] = no_taps
    taps[PIXELS : PIXELS + W_PAD, :C_MID] = no_taps

    def velocity_copy(kind, ref, slot, device):
        return pltpu.make_async_remote_copy(
            src_ref=ref,
            dst_ref=ref,
            send_sem=send_vel.at[kind, slot[0]],
            recv_sem=recv_vel.at[kind, slot[1]],
            device_id=device,
            device_id_type=MESH,
        )

    load_second.wait()
    spread_pixels(second_vmem, second_pix)

    def step_second(chunk):
        start = chunk * CHUNK
        out_grad = padded_chunk(grad_vmem, chunk)
        second = second_pix[pl.ds(start, CHUNK), :]
        back = dot(out_grad, w_third[...], 1, 1) * scale_three
        both = jnp.where(second > 0, back[:, :128], 0.0).astype(BF16)
        last = jnp.where(second[:, :C_MID] > 0, back[:, 128:], 0.0).astype(BF16)
        taps[pl.ds(start, CHUNK), :C_MID] = both[:, :C_MID]
        taps[pl.ds(start + W_PAD, CHUNK), C_MID : 2 * C_MID] = both[:, C_MID:]
        taps[pl.ds(start + 2 * W_PAD, CHUNK), 2 * C_MID :] = last
        sum_three[...] += dot(second[:, :C_MID].astype(BF16), out_grad, 0, 0)

    load_grad.wait()
    each_chunk(step_second)

    def place(columns, values):
        local[:, :, columns : columns + values.shape[1]] = values.reshape(
            groups, group_rows, values.shape[1]
        )

    def part_copy(index, columns, peer, slot, device):
        return pltpu.make_async_remote_copy(
            src_ref=local.at[peer, :, pl.ds(*columns)],
            dst_ref=got_one.at[slot, :, pl.ds(*columns)],
            send_sem=send_one.at[index, peer],
            recv_sem=recv_one.at[index, slot],
            device_id=device,
            device_id_type=MESH,
        )

    def send_part(index):
        for peer, device, peer_x, peer_core in group_peers:
            part_copy(index, PARTS[index], peer, my_group, device).start()

    place(AT_W3, sum_three[...] * (scale_three * mean_factor))

    load_first.wait()
    spread_pixels(first_vmem, first_pix)

    low = lax.broadcasted_iota(jnp.int32, (CHUNK, 128), 1) < 64

    def step_first(chunk):
        start = chunk * CHUNK
        first = first_pix[pl.ds(start, CHUNK), :]
        tap = taps[pl.ds(start + W_PAD, CHUNK), :]
        shifted = jnp.concatenate(
            [
                jnp.where(low, pltpu.roll(first, 1, 0), first),
                pltpu.roll(first, CHUNK - 1, 0)[:, :C_MID],
            ],
            axis=1,
        ).astype(BF16)
        sum_two[...] += dot(tap, shifted, 0, 0)
        spread = dot(tap, w_second[...], 1, 0)
        mixed = (
            pltpu.roll(spread[:, :128], CHUNK - 1, 0)[:, :C_MID]
            + spread[:, C_MID : 2 * C_MID]
            + pltpu.roll(spread[:, 128:], 1, 0)
        ) * scale_two
        back = jnp.where(first[:, :C_MID] > 0, mixed, 0.0).astype(BF16)
        back_first[pl.ds(start, CHUNK), :] = back
        sum_one[...] += dot(back, padded_chunk(x_vmem, chunk), 0, 0)

    load_x.wait()
    each_chunk(step_first)

    for tap_row in range(3):
        place(
            AT_W2 + 3 * C_MID * tap_row,
            sum_two[C_MID * tap_row : C_MID * (tap_row + 1), :] * (scale_two * mean_factor),
        )
    local[:, :, K_ROW:] = jnp.zeros((groups, group_rows, K_PAD - K_ROW), F32)
    place(AT_W1, sum_one[...] * (scale_one * mean_factor))
    load_velocity.wait()
    velocities[my_x, my_y, my_core] = velocity[...]
    pl.semaphore_wait(barrier, len(everyone))
    send_part(0)
    for peer, device in y_peers:
        velocity_copy(0, velocities.at[my_x, my_y, my_core], (peer, my_y), device).start()

    def step_input(chunk):
        start = chunk * CHUNK
        rise = dot(back_first[pl.ds(start, CHUNK), :], w_first[...], 1, 0) * scale_one
        rise = rise.reshape(H_CHUNK, W_PAD, C_IN)[:, :W_IMG]
        rows = rows_of(chunk)
        input_grad[0, rows] = (grad_vmem[rows].astype(F32) + rise).astype(BF16)

    each_chunk(step_input)

    block = local[my_group]
    for peer, device, peer_x, peer_core in group_peers:
        for index in range(len(PARTS)):
            part_copy(index, PARTS[index], peer, peer, device).wait_recv()
        block = block + got_one[peer]
    for index in range(size_y):
        rows_two[index] = block[index * own_rows : (index + 1) * own_rows]

    def two_copy(peer, slot, device):
        return pltpu.make_async_remote_copy(
            src_ref=rows_two.at[peer],
            dst_ref=got_two.at[slot],
            send_sem=send_two.at[peer],
            recv_sem=recv_two.at[slot],
            device_id=device,
            device_id_type=MESH,
        )

    for peer, device in y_peers:
        two_copy(peer, my_y, device).start()

    for peer, device in y_peers:
        velocity_copy(0, velocities.at[my_x, peer, my_core], (peer, peer), device).wait_recv()
    for peer, device, peer_x, peer_core in group_peers:
        velocity_copy(1, velocities.at[my_x, :, my_core], (peer, my_group), device).start()

    row = rows_two[my_y]
    for peer, device in y_peers:
        two_copy(peer, peer, device).wait_recv()
        row = row + got_two[peer]

    def three_copy(slot, peer, device):
        return pltpu.make_async_remote_copy(
            src_ref=got_three.at[slot],
            dst_ref=got_three.at[slot],
            send_sem=send_three.at[peer],
            recv_sem=recv_three.at[slot],
            device_id=device,
            device_id_type=MESH,
        )

    got_three[my_z] = row
    for peer, device in z_peers:
        three_copy(my_z, peer, device).start()
    for peer, device in z_peers:
        three_copy(peer, peer, device).wait_recv()
    row = got_three[0]
    for index in range(1, size_z):
        row = row + got_three[index]

    def four_copy(slot, peer, device):
        return pltpu.make_async_remote_copy(
            src_ref=rows_four.at[slot],
            dst_ref=rows_four.at[slot],
            send_sem=send_four.at[peer],
            recv_sem=recv_four.at[slot],
            device_id=device,
            device_id_type=MESH,
        )

    rows_four[my_y] = row
    for peer, device in y_peers:
        four_copy(my_y, peer, device).start()

    for peer, device, peer_x, peer_core in group_peers:
        other = velocities.at[peer_x, :, peer_core]
        velocity_copy(1, other, (peer, peer), device).wait_recv()
    for at_x in range(size_x):
        for at_y in range(size_y):
            for at_core in range(CORES):
                index = (at_x * size_y + at_y) * CORES + at_core
                velocity_flat[index * own_rows : (index + 1) * own_rows, :] = velocities[
                    at_x, at_y, at_core
                ]
    bounds = (
        (0, C_IN, AT_W1),
        (C_IN, C_IN + 9 * C_MID, AT_W2),
        (C_IN + 9 * C_MID, K_ROW, AT_W3),
    )
    weight_norms = [jnp.sqrt(total(params[:, low_end:high_end])) for low_end, high_end, _ in bounds]

    for peer, device in y_peers:
        four_copy(peer, peer, device).wait_recv()
    for index in range(size_y):
        grads[my_group, index * own_rows : (index + 1) * own_rows, :] = rows_four[index]

    def five_copy(slot, sent, device):
        return pltpu.make_async_remote_copy(
            src_ref=grads.at[slot],
            dst_ref=grads.at[slot],
            send_sem=send_five.at[sent],
            recv_sem=recv_five.at[slot],
            device_id=device,
            device_id_type=MESH,
        )

    sibling = group_peers[0]
    same_core = [peer for peer in group_peers[1::2]]
    far_first = sorted(range(len(same_core)), key=lambda at: -min(at + 1, size_x - 1 - at))
    for at in far_first:
        five_copy(my_group, same_core[at][0], same_core[at][1]).start()
    sent_five = [five_copy(my_group, peer[0], peer[1]) for peer in same_core]
    own = five_copy(my_group, sibling[0], sibling[1])
    own.start()
    sent_five.append(own)
    for at in far_first[::-1]:
        slot = same_core[at][0]
        five_copy(slot, slot, same_core[at][1]).wait_recv()
        onward = five_copy(slot, group_peers[2 * at + 2][0], sibling[1])
        onward.start()
        sent_five.append(onward)
    for peer in group_peers[::2]:
        five_copy(peer[0], peer[0], sibling[1]).wait_recv()

    for (low_end, high_end, column), weight_norm in zip(bounds, weight_norms):
        grad = grads[:, :, column : column + high_end - low_end].reshape(
            C_MID, high_end - low_end
        )
        rate = learn_rate * (weight_norm / (jnp.sqrt(total(grad)) + norm_eps))
        fresh = momentum * velocity_flat[:, low_end:high_end] + rate * grad
        velocity_flat[:, low_end:high_end] = fresh
        next_weights[:, low_end:high_end] = params[:, low_end:high_end] - fresh
    new_velocity[...] = velocity_flat[pl.ds(gx * own_rows, own_rows), :]

    for peer, device, peer_x, peer_core in group_peers:
        for index in range(len(PARTS)):
            part_copy(index, PARTS[index], peer, my_group, device).wait_send()
        velocity_copy(1, velocities.at[my_x, :, my_core], (peer, my_group), device).wait_send()
    for peer, device in y_peers:
        velocity_copy(0, velocities.at[my_x, my_y, my_core], (peer, my_y), device).wait_send()
        two_copy(peer, my_y, device).wait_send()
        four_copy(my_y, peer, device).wait_send()
    for peer, device in z_peers:
        three_copy(my_z, peer, device).wait_send()
    for copy in sent_five:
        copy.wait_send()


def shards(size_x, size_y, size_z, block_input, mid_first, mid_second, out_grad, params, velocity):
    groups = size_x * CORES
    group_rows = C_MID // groups
    own_rows = group_rows // size_y
    dma = pltpu.SemaphoreType.DMA
    return pl.pallas_call(
        functools.partial(kernel, size_x, size_y, size_z),
        out_shape=(
            pltpu.VMEM((1, H_DEV, W_IMG, C_IN), BF16),
            pltpu.VMEM((own_rows, K_ROW), F32),
            pltpu.VMEM((C_MID, K_ROW), F32),
        ),
        in_specs=[pl.BlockSpec(memory_space=pl.ANY)] * 6,
        out_specs=(pl.BlockSpec(memory_space=pltpu.VMEM),) * 3,
        scratch_shapes=[
            pltpu.VMEM((H_DEV, W_IMG, C_IN), BF16),
            pltpu.VMEM((H_DEV, W_IMG * C_MID), BF16),
            pltpu.VMEM((H_DEV, W_IMG * C_MID), BF16),
            pltpu.VMEM((H_DEV, W_IMG, C_IN), BF16),
            pltpu.VMEM((C_MID, K_ROW), F32),
            pltpu.VMEM((own_rows, K_ROW), F32),
            pltpu.VMEM((PIXELS, 128), F32),
            pltpu.VMEM((PIXELS, 128), F32),
            pltpu.VMEM((PIXELS + 2 * W_PAD, 3 * C_MID), BF16),
            pltpu.VMEM((PIXELS, C_MID), BF16),
            pltpu.VMEM((C_MID, C_IN), BF16),
            pltpu.VMEM((3 * C_MID, 3 * C_MID), BF16),
            pltpu.VMEM((3 * C_MID, C_IN), BF16),
            pltpu.VMEM((C_MID, C_IN), F32),
            pltpu.VMEM((3 * C_MID, 3 * C_MID), F32),
            pltpu.VMEM((C_MID, C_IN), F32),
            pltpu.VMEM((groups, group_rows, K_PAD), F32),
            pltpu.VMEM((groups, group_rows, K_PAD), F32),
            pltpu.VMEM((size_y, own_rows, K_PAD), F32),
            pltpu.VMEM((size_y, own_rows, K_PAD), F32),
            pltpu.VMEM((size_z, own_rows, K_PAD), F32),
            pltpu.VMEM((size_y, own_rows, K_PAD), F32),
            pltpu.VMEM((groups, group_rows, K_PAD), F32),
            pltpu.VMEM((size_x, size_y, CORES, own_rows, K_ROW), F32),
            pltpu.VMEM((C_MID, K_ROW), F32),
            dma((6,)),
            dma((len(PARTS), groups)),
            dma((len(PARTS), groups)),
            dma((size_y,)),
            dma((size_y,)),
            dma((size_z,)),
            dma((size_z,)),
            dma((size_y,)),
            dma((size_y,)),
            dma((groups,)),
            dma((groups,)),
            dma((2, max(groups, size_y))),
            dma((2, max(groups, size_y))),
        ],
        compiler_params=pltpu.CompilerParams(
            collective_id=0, has_side_effects=True, vmem_limit_bytes=62 * 1024 * 1024
        ),
        name="bottleneck_backward",
    )(block_input, mid_first, mid_second, out_grad, params, velocity)


def solution(mesh):
    return jax.shard_map(
        functools.partial(shards, ROWS_X, ROWS_Y, mesh.shape["gy"]),
        mesh=mesh,
        in_specs=(
            P(("gx", "gy"), None, None, None),
            P(("gx", "gy"), None, None),
            P(("gx", "gy"), None, None),
            P(("gx", "gy"), None, None, None),
            P(),
            P("gx", None),
        ),
        out_specs=(P(("gx", "gy"), None, None, None), P("gx", None), P()),
        check_vma=False,
    )
```

```python
import functools
import math

import jax
import jax.numpy as jnp
from jax import lax
from jax.experimental import pallas as pl
from jax.experimental.pallas import tpu as pltpu
from jax.sharding import PartitionSpec as P

C_IN = 256
C_MID = 64
H_DEV = 40
W_IMG = 56
W_PAD = 64
K_ROW = 1088
K_PAD = 1152
PIXELS = H_DEV * W_PAD
ROWS_X = 4
ROWS_Y = 8
CORES = 2

H_CHUNK = 8
CHUNK = H_CHUNK * W_PAD
CHUNKS = H_DEV // H_CHUNK

learn_rate = 0.5
momentum = 0.9
norm_eps = 1e-06

F32 = jnp.float32
BF16 = jnp.bfloat16
MESH = pl.DeviceIdType.MESH

AT_W3 = 0
AT_W1 = 256
AT_W2 = 512


def dot(left, right, left_dim, right_dim):
    return lax.dot_general(
        left, right, (((left_dim,), (right_dim,)), ((), ())), preferred_element_type=F32
    )


def spread_pixels(fields, out):
    low = lax.broadcasted_iota(jnp.int32, (H_DEV, 128), 1) < 64
    for pair in range(W_IMG // 2):
        both = fields[:, 128 * pair : 128 * (pair + 1)].astype(F32)
        swapped = pltpu.roll(both, 64, 1)
        out[pl.ds(2 * pair, H_DEV, stride=W_PAD), :] = jnp.where(low, both, swapped)
        out[pl.ds(2 * pair + 1, H_DEV, stride=W_PAD), :] = jnp.where(low, swapped, both)
    zeros = jnp.zeros((W_PAD - W_IMG, 128), F32)
    for row in range(H_DEV):
        out[row * W_PAD + W_IMG : (row + 1) * W_PAD, :] = zeros


def padded_chunk(ref, chunk):
    values = ref[chunk * H_CHUNK : (chunk + 1) * H_CHUNK].astype(F32)
    zeros = jnp.zeros((H_CHUNK, W_PAD - W_IMG, C_IN), F32)
    return jnp.concatenate([values, zeros], axis=1).reshape(CHUNK, C_IN).astype(BF16)


def each_chunk(step):
    for chunk in range(CHUNKS):
        step(chunk)


def total(values):
    return jnp.sum(jnp.sum(values * values, axis=0, keepdims=True), axis=1, keepdims=True)


def kernel(
    size_x,
    size_y,
    size_z,
    x_hbm,
    first_hbm,
    second_hbm,
    grad_hbm,
    params_hbm,
    velocity_hbm,
    input_grad,
    new_velocity,
    next_weights,
    x_vmem,
    first_vmem,
    second_vmem,
    grad_vmem,
    params,
    velocity,
    first_pix,
    second_pix,
    taps,
    back_first,
    w_first,
    w_second,
    w_third,
    sum_one,
    sum_two,
    sum_three,
    local,
    got_pair,
    pairs,
    got_one,
    rows_two,
    got_two,
    got_three,
    rows_four,
    grads,
    velocities,
    velocity_flat,
    load_sem,
    send_pair,
    recv_pair,
    send_one,
    recv_one,
    send_two,
    recv_two,
    send_three,
    recv_three,
    send_four,
    recv_four,
    send_five,
    recv_five,
    send_vel,
    recv_vel,
):
    groups = size_x * CORES
    group_rows = C_MID // groups
    own_rows = group_rows // size_y
    strips = groups * size_y * size_z
    scale_one = 1.0 / math.sqrt(C_IN)
    scale_two = 1.0 / math.sqrt(9 * C_MID)
    scale_three = 1.0 / math.sqrt(C_MID)
    mean_factor = 1.0 / strips

    def rows_of(chunk):
        return pl.ds(chunk * H_CHUNK, H_CHUNK)

    def load(src, dst, slot):
        copy = pltpu.make_async_copy(src, dst, load_sem.at[slot])
        copy.start()
        return copy

    load_params = load(params_hbm, params, 0)
    load_second = load(second_hbm.at[0], second_vmem, 1)
    load_grad = load(grad_hbm.at[0], grad_vmem, 2)
    load_first = load(first_hbm.at[0], first_vmem, 3)
    load_x = load(x_hbm.at[0], x_vmem, 4)
    load_velocity = load(velocity_hbm, velocity, 5)

    gx = lax.axis_index("gx")
    my_z = lax.axis_index("gy")
    my_core = lax.rem(gx, CORES)
    my_y = lax.rem(gx // CORES, size_y)
    my_x = gx // (CORES * size_y)
    my_group = my_x * CORES + my_core

    def wrap(index, size):
        return jnp.where(index >= size, index - size, index)

    group_peers = []
    for step in range(size_x):
        peer_x = wrap(my_x + step, size_x)
        for core in (my_core, 1 - my_core) if step else (1 - my_core,):
            index = (peer_x * size_y + my_y) * CORES + core
            group_peers.append((peer_x * CORES + core, (index, my_z), peer_x, core))
    def far_first(size):
        return sorted(range(1, size), key=lambda step: -min(step, size - step))

    y_peers = []
    for step in far_first(size_y):
        peer = wrap(my_y + step, size_y)
        y_peers.append((peer, ((my_x * size_y + peer) * CORES + my_core, my_z)))
    z_peers = []
    for step in far_first(size_z):
        peer = wrap(my_z + step, size_z)
        z_peers.append((peer, (gx, peer)))

    barrier = pltpu.get_barrier_semaphore()
    everyone = [peer[1] for peer in group_peers + y_peers + z_peers]
    for device in everyone:
        pl.semaphore_signal(barrier, inc=1, device_id=device, device_id_type=MESH)

    load_params.wait()
    weights = params[...].astype(BF16)
    w_first[...] = weights[:, :C_IN]
    for tap_row in range(3):
        start = C_IN + 3 * C_MID * tap_row
        w_second[C_MID * tap_row : C_MID * (tap_row + 1), :] = weights[:, start : start + 3 * C_MID]
        w_third[C_MID * tap_row : C_MID * (tap_row + 1), :] = weights[:, C_IN + 9 * C_MID :]

    sum_one[...] = jnp.zeros_like(sum_one)
    sum_two[...] = jnp.zeros_like(sum_two)
    sum_three[...] = jnp.zeros_like(sum_three)
    no_taps = jnp.zeros((W_PAD, C_MID), BF16)
    taps[W_PAD : 2 * W_PAD, 2 * C_MID :] = no_taps
    taps[PIXELS : PIXELS + W_PAD, :C_MID] = no_taps

    def velocity_copy(kind, ref, slot, device):
        return pltpu.make_async_remote_copy(
            src_ref=ref,
            dst_ref=ref,
            send_sem=send_vel.at[kind, slot[0]],
            recv_sem=recv_vel.at[kind, slot[1]],
            device_id=device,
            device_id_type=MESH,
        )

    load_second.wait()
    spread_pixels(second_vmem, second_pix)

    def step_second(chunk):
        start = chunk * CHUNK
        out_grad = padded_chunk(grad_vmem, chunk)
        second = second_pix[pl.ds(start, CHUNK), :]
        back = dot(out_grad, w_third[...], 1, 1) * scale_three
        both = jnp.where(second > 0, back[:, :128], 0.0).astype(BF16)
        last = jnp.where(second[:, :C_MID] > 0, back[:, 128:], 0.0).astype(BF16)
        taps[pl.ds(start, CHUNK), :C_MID] = both[:, :C_MID]
        taps[pl.ds(start + W_PAD, CHUNK), C_MID : 2 * C_MID] = both[:, C_MID:]
        taps[pl.ds(start + 2 * W_PAD, CHUNK), 2 * C_MID :] = last
        sum_three[...] += dot(second[:, :C_MID].astype(BF16), out_grad, 0, 0)

    load_grad.wait()
    each_chunk(step_second)

    def place(columns, values):
        local[:, :, columns : columns + values.shape[1]] = values.reshape(
            groups, group_rows, values.shape[1]
        )

    place(AT_W3, sum_three[...] * (scale_three * mean_factor))

    sibling = group_peers[0]
    same_core = [group_peers[2 * step - 1] for step in far_first(size_x)]
    other_core = [group_peers[2 * step] for step in far_first(size_x)] + [sibling]

    def pair_copy(at_x, core):
        return pltpu.make_async_remote_copy(
            src_ref=local.at[at_x * CORES + core],
            dst_ref=got_pair.at[at_x],
            send_sem=send_pair.at[at_x],
            recv_sem=recv_pair.at[at_x],
            device_id=sibling[1],
            device_id_type=MESH,
        )

    def one_copy(at_x, slot, device):
        return pltpu.make_async_remote_copy(
            src_ref=pairs.at[at_x],
            dst_ref=got_one.at[slot],
            send_sem=send_one.at[at_x],
            recv_sem=recv_one.at[slot],
            device_id=device,
            device_id_type=MESH,
        )

    load_first.wait()
    spread_pixels(first_vmem, first_pix)

    low = lax.broadcasted_iota(jnp.int32, (CHUNK, 128), 1) < 64

    def step_first(chunk):
        start = chunk * CHUNK
        first = first_pix[pl.ds(start, CHUNK), :]
        tap = taps[pl.ds(start + W_PAD, CHUNK), :]
        shifted = jnp.concatenate(
            [
                jnp.where(low, pltpu.roll(first, 1, 0), first),
                pltpu.roll(first, CHUNK - 1, 0)[:, :C_MID],
            ],
            axis=1,
        ).astype(BF16)
        sum_two[...] += dot(tap, shifted, 0, 0)
        spread = dot(tap, w_second[...], 1, 0)
        mixed = (
            pltpu.roll(spread[:, :128], CHUNK - 1, 0)[:, :C_MID]
            + spread[:, C_MID : 2 * C_MID]
            + pltpu.roll(spread[:, 128:], 1, 0)
        ) * scale_two
        back = jnp.where(first[:, :C_MID] > 0, mixed, 0.0).astype(BF16)
        back_first[pl.ds(start, CHUNK), :] = back
        sum_one[...] += dot(back, padded_chunk(x_vmem, chunk), 0, 0)

    load_x.wait()
    each_chunk(step_first)

    for tap_row in range(3):
        place(
            AT_W2 + 3 * C_MID * tap_row,
            sum_two[C_MID * tap_row : C_MID * (tap_row + 1), :] * (scale_two * mean_factor),
        )
    local[:, :, K_ROW:] = jnp.zeros((groups, group_rows, K_PAD - K_ROW), F32)
    place(AT_W1, sum_one[...] * (scale_one * mean_factor))
    load_velocity.wait()
    velocities[my_x, my_y, my_core] = velocity[...]
    pl.semaphore_wait(barrier, len(everyone))
    for peer in other_core:
        pair_copy(peer[2], peer[3]).start()
    for peer, device, peer_x, peer_core in same_core:
        pair_copy(peer_x, my_core).wait_recv()
        pairs[peer_x] = local[peer] + got_pair[peer_x]
        one_copy(peer_x, my_x, device).start()
    for peer, device in y_peers:
        velocity_copy(0, velocities.at[my_x, my_y, my_core], (peer, my_y), device).start()

    def step_input(chunk):
        start = chunk * CHUNK
        rise = dot(back_first[pl.ds(start, CHUNK), :], w_first[...], 1, 0) * scale_one
        rise = rise.reshape(H_CHUNK, W_PAD, C_IN)[:, :W_IMG]
        rows = rows_of(chunk)
        input_grad[0, rows] = (grad_vmem[rows].astype(F32) + rise).astype(BF16)

    each_chunk(step_input)

    pair_copy(my_x, my_core).wait_recv()
    block = local[my_group] + got_pair[my_x]
    for peer, device, peer_x, peer_core in same_core[::-1]:
        one_copy(peer_x, peer_x, device).wait_recv()
        block = block + got_one[peer_x]
    for index in range(size_y):
        rows_two[index] = block[index * own_rows : (index + 1) * own_rows]

    def two_copy(peer, slot, device):
        return pltpu.make_async_remote_copy(
            src_ref=rows_two.at[peer],
            dst_ref=got_two.at[slot],
            send_sem=send_two.at[peer],
            recv_sem=recv_two.at[slot],
            device_id=device,
            device_id_type=MESH,
        )

    for peer, device in y_peers:
        two_copy(peer, my_y, device).start()

    for peer, device in y_peers:
        velocity_copy(0, velocities.at[my_x, peer, my_core], (peer, peer), device).wait_recv()
    for peer, device, peer_x, peer_core in group_peers:
        velocity_copy(1, velocities.at[my_x, :, my_core], (peer, my_group), device).start()

    row = rows_two[my_y]
    for peer, device in y_peers[::-1]:
        two_copy(peer, peer, device).wait_recv()
        row = row + got_two[peer]

    def three_copy(slot, peer, device):
        return pltpu.make_async_remote_copy(
            src_ref=got_three.at[slot],
            dst_ref=got_three.at[slot],
            send_sem=send_three.at[peer],
            recv_sem=recv_three.at[slot],
            device_id=device,
            device_id_type=MESH,
        )

    got_three[my_z] = row
    for peer, device in z_peers:
        three_copy(my_z, peer, device).start()
    for peer, device in z_peers[::-1]:
        three_copy(peer, peer, device).wait_recv()
    row = got_three[0]
    for index in range(1, size_z):
        row = row + got_three[index]

    def four_copy(slot, peer, device):
        return pltpu.make_async_remote_copy(
            src_ref=rows_four.at[slot],
            dst_ref=rows_four.at[slot],
            send_sem=send_four.at[peer],
            recv_sem=recv_four.at[slot],
            device_id=device,
            device_id_type=MESH,
        )

    rows_four[my_y] = row
    for peer, device in y_peers:
        four_copy(my_y, peer, device).start()

    for peer, device, peer_x, peer_core in group_peers:
        other = velocities.at[peer_x, :, peer_core]
        velocity_copy(1, other, (peer, peer), device).wait_recv()
    for at_x in range(size_x):
        for at_y in range(size_y):
            for at_core in range(CORES):
                index = (at_x * size_y + at_y) * CORES + at_core
                velocity_flat[index * own_rows : (index + 1) * own_rows, :] = velocities[
                    at_x, at_y, at_core
                ]
    bounds = (
        (0, C_IN, AT_W1),
        (C_IN, C_IN + 9 * C_MID, AT_W2),
        (C_IN + 9 * C_MID, K_ROW, AT_W3),
    )
    weight_norms = [jnp.sqrt(total(params[:, low_end:high_end])) for low_end, high_end, _ in bounds]

    for peer, device in y_peers[::-1]:
        four_copy(peer, peer, device).wait_recv()
    for index in range(size_y):
        grads[my_group, index * own_rows : (index + 1) * own_rows, :] = rows_four[index]

    def five_copy(slot, sent, device):
        return pltpu.make_async_remote_copy(
            src_ref=grads.at[slot],
            dst_ref=grads.at[slot],
            send_sem=send_five.at[sent],
            recv_sem=recv_five.at[slot],
            device_id=device,
            device_id_type=MESH,
        )

    sent_five = []

    def send_five_to(slot, sent, device):
        copy = five_copy(slot, sent, device)
        copy.start()
        sent_five.append(copy)

    for peer in same_core:
        send_five_to(my_group, peer[0], peer[1])
    send_five_to(my_group, sibling[0], sibling[1])
    for here, there in zip(same_core[::-1], other_core[-2::-1]):
        five_copy(here[0], here[0], here[1]).wait_recv()
        send_five_to(here[0], there[0], sibling[1])
    for peer in group_peers[::2]:
        five_copy(peer[0], peer[0], sibling[1]).wait_recv()

    for (low_end, high_end, column), weight_norm in zip(bounds, weight_norms):
        grad = grads[:, :, column : column + high_end - low_end].reshape(
            C_MID, high_end - low_end
        )
        rate = learn_rate * (weight_norm / (jnp.sqrt(total(grad)) + norm_eps))
        fresh = momentum * velocity_flat[:, low_end:high_end] + rate * grad
        velocity_flat[:, low_end:high_end] = fresh
        next_weights[:, low_end:high_end] = params[:, low_end:high_end] - fresh
    new_velocity[...] = velocity_flat[pl.ds(gx * own_rows, own_rows), :]

    for peer, device, peer_x, peer_core in group_peers:
        velocity_copy(1, velocities.at[my_x, :, my_core], (peer, my_group), device).wait_send()
    for peer, device in y_peers:
        velocity_copy(0, velocities.at[my_x, my_y, my_core], (peer, my_y), device).wait_send()
        two_copy(peer, my_y, device).wait_send()
        four_copy(my_y, peer, device).wait_send()
    for peer, device in z_peers:
        three_copy(my_z, peer, device).wait_send()
    for peer in other_core:
        pair_copy(peer[2], peer[3]).wait_send()
    for peer, device, peer_x, peer_core in same_core:
        one_copy(peer_x, my_x, device).wait_send()
    for copy in sent_five:
        copy.wait_send()


def shards(size_x, size_y, size_z, block_input, mid_first, mid_second, out_grad, params, velocity):
    groups = size_x * CORES
    group_rows = C_MID // groups
    own_rows = group_rows // size_y
    dma = pltpu.SemaphoreType.DMA
    return pl.pallas_call(
        functools.partial(kernel, size_x, size_y, size_z),
        out_shape=(
            pltpu.VMEM((1, H_DEV, W_IMG, C_IN), BF16),
            pltpu.VMEM((own_rows, K_ROW), F32),
            pltpu.VMEM((C_MID, K_ROW), F32),
        ),
        in_specs=[pl.BlockSpec(memory_space=pl.ANY)] * 6,
        out_specs=(pl.BlockSpec(memory_space=pltpu.VMEM),) * 3,
        scratch_shapes=[
            pltpu.VMEM((H_DEV, W_IMG, C_IN), BF16),
            pltpu.VMEM((H_DEV, W_IMG * C_MID), BF16),
            pltpu.VMEM((H_DEV, W_IMG * C_MID), BF16),
            pltpu.VMEM((H_DEV, W_IMG, C_IN), BF16),
            pltpu.VMEM((C_MID, K_ROW), F32),
            pltpu.VMEM((own_rows, K_ROW), F32),
            pltpu.VMEM((PIXELS, 128), F32),
            pltpu.VMEM((PIXELS, 128), F32),
            pltpu.VMEM((PIXELS + 2 * W_PAD, 3 * C_MID), BF16),
            pltpu.VMEM((PIXELS, C_MID), BF16),
            pltpu.VMEM((C_MID, C_IN), BF16),
            pltpu.VMEM((3 * C_MID, 3 * C_MID), BF16),
            pltpu.VMEM((3 * C_MID, C_IN), BF16),
            pltpu.VMEM((C_MID, C_IN), F32),
            pltpu.VMEM((3 * C_MID, 3 * C_MID), F32),
            pltpu.VMEM((C_MID, C_IN), F32),
            pltpu.VMEM((groups, group_rows, K_PAD), F32),
            pltpu.VMEM((size_x, group_rows, K_PAD), F32),
            pltpu.VMEM((size_x, group_rows, K_PAD), F32),
            pltpu.VMEM((size_x, group_rows, K_PAD), F32),
            pltpu.VMEM((size_y, own_rows, K_PAD), F32),
            pltpu.VMEM((size_y, own_rows, K_PAD), F32),
            pltpu.VMEM((size_z, own_rows, K_PAD), F32),
            pltpu.VMEM((size_y, own_rows, K_PAD), F32),
            pltpu.VMEM((groups, group_rows, K_PAD), F32),
            pltpu.VMEM((size_x, size_y, CORES, own_rows, K_ROW), F32),
            pltpu.VMEM((C_MID, K_ROW), F32),
            dma((6,)),
            dma((size_x,)),
            dma((size_x,)),
            dma((size_x,)),
            dma((size_x,)),
            dma((size_y,)),
            dma((size_y,)),
            dma((size_z,)),
            dma((size_z,)),
            dma((size_y,)),
            dma((size_y,)),
            dma((groups,)),
            dma((groups,)),
            dma((2, max(groups, size_y))),
            dma((2, max(groups, size_y))),
        ],
        compiler_params=pltpu.CompilerParams(
            collective_id=0, has_side_effects=True, vmem_limit_bytes=62 * 1024 * 1024
        ),
        name="bottleneck_backward",
    )(block_input, mid_first, mid_second, out_grad, params, velocity)


def solution(mesh):
    return jax.shard_map(
        functools.partial(shards, ROWS_X, ROWS_Y, mesh.shape["gy"]),
        mesh=mesh,
        in_specs=(
            P(("gx", "gy"), None, None, None),
            P(("gx", "gy"), None, None),
            P(("gx", "gy"), None, None),
            P(("gx", "gy"), None, None, None),
            P(),
            P("gx", None),
        ),
        out_specs=(P(("gx", "gy"), None, None, None), P("gx", None), P()),
        check_vma=False,
    )
```

```python
import functools
import math

import jax
import jax.numpy as jnp
from jax import lax
from jax.experimental import pallas as pl
from jax.experimental.pallas import tpu as pltpu
from jax.sharding import PartitionSpec as P

C_IN = 256
C_MID = 64
H_DEV = 40
W_IMG = 56
W_PAD = 64
K_ROW = 1088
K_PAD = 1152
PIXELS = H_DEV * W_PAD
ROWS_X = 4
ROWS_Y = 8
CORES = 2

H_CHUNK = 40
CHUNK = H_CHUNK * W_PAD
CHUNKS = H_DEV // H_CHUNK

learn_rate = 0.5
momentum = 0.9
norm_eps = 1e-06

F32 = jnp.float32
BF16 = jnp.bfloat16
MESH = pl.DeviceIdType.MESH

AT_W3 = 0
AT_W1 = 256
AT_W2 = 512


def dot(left, right, left_dim, right_dim):
    return lax.dot_general(
        left, right, (((left_dim,), (right_dim,)), ((), ())), preferred_element_type=F32
    )


def spread_pixels(fields, out):
    low = lax.broadcasted_iota(jnp.int32, (H_DEV, 128), 1) < 64
    for pair in range(W_IMG // 2):
        both = fields[:, 128 * pair : 128 * (pair + 1)].astype(F32)
        swapped = pltpu.roll(both, 64, 1)
        out[pl.ds(2 * pair, H_DEV, stride=W_PAD), :] = jnp.where(low, both, swapped)
        out[pl.ds(2 * pair + 1, H_DEV, stride=W_PAD), :] = jnp.where(low, swapped, both)
    zeros = jnp.zeros((W_PAD - W_IMG, 128), F32)
    for row in range(H_DEV):
        out[row * W_PAD + W_IMG : (row + 1) * W_PAD, :] = zeros


def padded_chunk(ref, chunk):
    values = ref[chunk * H_CHUNK : (chunk + 1) * H_CHUNK].astype(F32)
    zeros = jnp.zeros((H_CHUNK, W_PAD - W_IMG, C_IN), F32)
    return jnp.concatenate([values, zeros], axis=1).reshape(CHUNK, C_IN).astype(BF16)


def each_chunk(step):
    for chunk in range(CHUNKS):
        step(chunk)


def total(values):
    return jnp.sum(jnp.sum(values * values, axis=0, keepdims=True), axis=1, keepdims=True)


def kernel(
    size_x,
    size_y,
    size_z,
    x_hbm,
    first_hbm,
    second_hbm,
    grad_hbm,
    params_hbm,
    velocity_hbm,
    input_grad,
    new_velocity,
    next_weights,
    x_vmem,
    first_vmem,
    second_vmem,
    grad_vmem,
    params,
    velocity,
    first_pix,
    second_pix,
    taps,
    back_first,
    w_first,
    w_second,
    w_third,
    sum_one,
    sum_two,
    sum_three,
    local,
    got_pair,
    pairs,
    got_one,
    rows_two,
    got_two,
    got_three,
    rows_four,
    grads,
    velocities,
    velocity_flat,
    load_sem,
    send_pair,
    recv_pair,
    send_one,
    recv_one,
    send_two,
    recv_two,
    send_three,
    recv_three,
    send_four,
    recv_four,
    send_five,
    recv_five,
    send_vel,
    recv_vel,
):
    groups = size_x * CORES
    group_rows = C_MID // groups
    own_rows = group_rows // size_y
    strips = groups * size_y * size_z
    scale_one = 1.0 / math.sqrt(C_IN)
    scale_two = 1.0 / math.sqrt(9 * C_MID)
    scale_three = 1.0 / math.sqrt(C_MID)
    mean_factor = 1.0 / strips

    def rows_of(chunk):
        return pl.ds(chunk * H_CHUNK, H_CHUNK)

    def load(src, dst, slot):
        copy = pltpu.make_async_copy(src, dst, load_sem.at[slot])
        copy.start()
        return copy

    load_params = load(params_hbm, params, 0)
    load_second = load(second_hbm.at[0], second_vmem, 1)
    load_grad = load(grad_hbm.at[0], grad_vmem, 2)
    load_first = load(first_hbm.at[0], first_vmem, 3)
    load_x = load(x_hbm.at[0], x_vmem, 4)
    load_velocity = load(velocity_hbm, velocity, 5)

    gx = lax.axis_index("gx")
    my_z = lax.axis_index("gy")
    my_core = lax.rem(gx, CORES)
    my_y = lax.rem(gx // CORES, size_y)
    my_x = gx // (CORES * size_y)
    my_group = my_x * CORES + my_core

    def wrap(index, size):
        return jnp.where(index >= size, index - size, index)

    group_peers = []
    for step in range(size_x):
        peer_x = wrap(my_x + step, size_x)
        for core in (my_core, 1 - my_core) if step else (1 - my_core,):
            index = (peer_x * size_y + my_y) * CORES + core
            group_peers.append((peer_x * CORES + core, (index, my_z), peer_x, core))
    def far_first(size):
        return sorted(range(1, size), key=lambda step: -min(step, size - step))

    y_peers = []
    for step in far_first(size_y):
        peer = wrap(my_y + step, size_y)
        y_peers.append((peer, ((my_x * size_y + peer) * CORES + my_core, my_z)))
    z_peers = []
    for step in far_first(size_z):
        peer = wrap(my_z + step, size_z)
        z_peers.append((peer, (gx, peer)))

    barrier = pltpu.get_barrier_semaphore()
    everyone = [peer[1] for peer in z_peers + y_peers + group_peers]
    for device in everyone:
        pl.semaphore_signal(barrier, inc=1, device_id=device, device_id_type=MESH)

    load_params.wait()
    weights = params[...].astype(BF16)
    w_first[...] = weights[:, :C_IN]
    for tap_row in range(3):
        start = C_IN + 3 * C_MID * tap_row
        w_second[C_MID * tap_row : C_MID * (tap_row + 1), :] = weights[:, start : start + 3 * C_MID]
        w_third[C_MID * tap_row : C_MID * (tap_row + 1), :] = weights[:, C_IN + 9 * C_MID :]

    sum_one[...] = jnp.zeros_like(sum_one)
    sum_two[...] = jnp.zeros_like(sum_two)
    sum_three[...] = jnp.zeros_like(sum_three)
    no_taps = jnp.zeros((W_PAD, C_MID), BF16)
    taps[W_PAD : 2 * W_PAD, 2 * C_MID :] = no_taps
    taps[PIXELS : PIXELS + W_PAD, :C_MID] = no_taps

    def velocity_copy(kind, ref, slot, device):
        return pltpu.make_async_remote_copy(
            src_ref=ref,
            dst_ref=ref,
            send_sem=send_vel.at[kind, slot[0]],
            recv_sem=recv_vel.at[kind, slot[1]],
            device_id=device,
            device_id_type=MESH,
        )

    load_second.wait()
    spread_pixels(second_vmem, second_pix)

    def step_second(chunk):
        start = chunk * CHUNK
        out_grad = padded_chunk(grad_vmem, chunk)
        second = second_pix[pl.ds(start, CHUNK), :]
        back = dot(out_grad, w_third[...], 1, 1) * scale_three
        both = jnp.where(second > 0, back[:, :128], 0.0).astype(BF16)
        last = jnp.where(second[:, :C_MID] > 0, back[:, 128:], 0.0).astype(BF16)
        taps[pl.ds(start, CHUNK), :C_MID] = both[:, :C_MID]
        taps[pl.ds(start + W_PAD, CHUNK), C_MID : 2 * C_MID] = both[:, C_MID:]
        taps[pl.ds(start + 2 * W_PAD, CHUNK), 2 * C_MID :] = last
        sum_three[...] += dot(second[:, :C_MID].astype(BF16), out_grad, 0, 0)

    load_grad.wait()
    each_chunk(step_second)

    def place(columns, values):
        local[:, :, columns : columns + values.shape[1]] = values.reshape(
            groups, group_rows, values.shape[1]
        )

    place(AT_W3, sum_three[...] * (scale_three * mean_factor))

    sibling = group_peers[0]
    same_core = [group_peers[2 * step - 1] for step in far_first(size_x)]
    other_core = [group_peers[2 * step] for step in far_first(size_x)] + [sibling]

    def pair_copy(at_x, core):
        return pltpu.make_async_remote_copy(
            src_ref=local.at[at_x * CORES + core],
            dst_ref=got_pair.at[at_x],
            send_sem=send_pair.at[at_x],
            recv_sem=recv_pair.at[at_x],
            device_id=sibling[1],
            device_id_type=MESH,
        )

    def one_copy(at_x, slot, device):
        return pltpu.make_async_remote_copy(
            src_ref=pairs.at[at_x],
            dst_ref=got_one.at[slot],
            send_sem=send_one.at[at_x],
            recv_sem=recv_one.at[slot],
            device_id=device,
            device_id_type=MESH,
        )

    load_first.wait()
    spread_pixels(first_vmem, first_pix)

    low = lax.broadcasted_iota(jnp.int32, (CHUNK, 128), 1) < 64

    def step_first(chunk):
        start = chunk * CHUNK
        first = first_pix[pl.ds(start, CHUNK), :]
        tap = taps[pl.ds(start + W_PAD, CHUNK), :]
        shifted = jnp.concatenate(
            [
                jnp.where(low, pltpu.roll(first, 1, 0), first),
                pltpu.roll(first, CHUNK - 1, 0)[:, :C_MID],
            ],
            axis=1,
        ).astype(BF16)
        sum_two[...] += dot(tap, shifted, 0, 0)
        spread = dot(tap, w_second[...], 1, 0)
        mixed = (
            pltpu.roll(spread[:, :128], CHUNK - 1, 0)[:, :C_MID]
            + spread[:, C_MID : 2 * C_MID]
            + pltpu.roll(spread[:, 128:], 1, 0)
        ) * scale_two
        back = jnp.where(first[:, :C_MID] > 0, mixed, 0.0).astype(BF16)
        back_first[pl.ds(start, CHUNK), :] = back
        sum_one[...] += dot(back, padded_chunk(x_vmem, chunk), 0, 0)

    load_x.wait()
    each_chunk(step_first)

    for tap_row in range(3):
        place(
            AT_W2 + 3 * C_MID * tap_row,
            sum_two[C_MID * tap_row : C_MID * (tap_row + 1), :] * (scale_two * mean_factor),
        )
    local[:, :, K_ROW:] = jnp.zeros((groups, group_rows, K_PAD - K_ROW), F32)
    place(AT_W1, sum_one[...] * (scale_one * mean_factor))
    load_velocity.wait()
    velocities[my_x, my_y, my_core] = velocity[...]
    pl.semaphore_wait(barrier, len(everyone))
    for peer in other_core:
        pair_copy(peer[2], peer[3]).start()
    for peer, device, peer_x, peer_core in same_core:
        pair_copy(peer_x, my_core).wait_recv()
        pairs[peer_x] = local[peer] + got_pair[peer_x]
        one_copy(peer_x, my_x, device).start()
    for peer, device in y_peers:
        velocity_copy(0, velocities.at[my_x, my_y, my_core], (peer, my_y), device).start()

    def step_input(chunk):
        start = chunk * CHUNK
        rise = dot(back_first[pl.ds(start, CHUNK), :], w_first[...], 1, 0) * scale_one
        rise = rise.reshape(H_CHUNK, W_PAD, C_IN)[:, :W_IMG]
        rows = rows_of(chunk)
        input_grad[0, rows] = (grad_vmem[rows].astype(F32) + rise).astype(BF16)

    each_chunk(step_input)

    pair_copy(my_x, my_core).wait_recv()
    block = local[my_group] + got_pair[my_x]
    for peer, device, peer_x, peer_core in same_core[::-1]:
        one_copy(peer_x, peer_x, device).wait_recv()
        block = block + got_one[peer_x]
    for index in range(size_y):
        rows_two[index] = block[index * own_rows : (index + 1) * own_rows]

    def two_copy(peer, slot, device):
        return pltpu.make_async_remote_copy(
            src_ref=rows_two.at[peer],
            dst_ref=got_two.at[slot],
            send_sem=send_two.at[peer],
            recv_sem=recv_two.at[slot],
            device_id=device,
            device_id_type=MESH,
        )

    for peer, device in y_peers:
        two_copy(peer, my_y, device).start()

    for peer, device in y_peers:
        velocity_copy(0, velocities.at[my_x, peer, my_core], (peer, peer), device).wait_recv()
    for peer, device, peer_x, peer_core in group_peers:
        velocity_copy(1, velocities.at[my_x, :, my_core], (peer, my_group), device).start()

    row = rows_two[my_y]
    for peer, device in y_peers[::-1]:
        two_copy(peer, peer, device).wait_recv()
        row = row + got_two[peer]

    def three_copy(slot, peer, device):
        return pltpu.make_async_remote_copy(
            src_ref=got_three.at[slot],
            dst_ref=got_three.at[slot],
            send_sem=send_three.at[peer],
            recv_sem=recv_three.at[slot],
            device_id=device,
            device_id_type=MESH,
        )

    got_three[my_z] = row
    for peer, device in z_peers:
        three_copy(my_z, peer, device).start()
    for peer, device in z_peers[::-1]:
        three_copy(peer, peer, device).wait_recv()
    row = got_three[0]
    for index in range(1, size_z):
        row = row + got_three[index]

    def four_copy(slot, peer, device):
        return pltpu.make_async_remote_copy(
            src_ref=rows_four.at[slot],
            dst_ref=rows_four.at[slot],
            send_sem=send_four.at[peer],
            recv_sem=recv_four.at[slot],
            device_id=device,
            device_id_type=MESH,
        )

    rows_four[my_y] = row
    for peer, device in y_peers:
        four_copy(my_y, peer, device).start()

    for peer, device, peer_x, peer_core in group_peers:
        other = velocities.at[peer_x, :, peer_core]
        velocity_copy(1, other, (peer, peer), device).wait_recv()
    for at_x in range(size_x):
        for at_y in range(size_y):
            for at_core in range(CORES):
                index = (at_x * size_y + at_y) * CORES + at_core
                velocity_flat[index * own_rows : (index + 1) * own_rows, :] = velocities[
                    at_x, at_y, at_core
                ]
    bounds = (
        (0, C_IN, AT_W1),
        (C_IN, C_IN + 9 * C_MID, AT_W2),
        (C_IN + 9 * C_MID, K_ROW, AT_W3),
    )
    weight_norms = [jnp.sqrt(total(params[:, low_end:high_end])) for low_end, high_end, _ in bounds]

    for peer, device in y_peers[::-1]:
        four_copy(peer, peer, device).wait_recv()
    for index in range(size_y):
        grads[my_group, index * own_rows : (index + 1) * own_rows, :] = rows_four[index]

    def five_copy(slot, sent, device):
        return pltpu.make_async_remote_copy(
            src_ref=grads.at[slot],
            dst_ref=grads.at[slot],
            send_sem=send_five.at[sent],
            recv_sem=recv_five.at[slot],
            device_id=device,
            device_id_type=MESH,
        )

    sent_five = []

    def send_five_to(slot, sent, device):
        copy = five_copy(slot, sent, device)
        copy.start()
        sent_five.append(copy)

    for peer in same_core:
        send_five_to(my_group, peer[0], peer[1])
    send_five_to(my_group, sibling[0], sibling[1])
    for here, there in zip(same_core[::-1], other_core[-2::-1]):
        five_copy(here[0], here[0], here[1]).wait_recv()
        send_five_to(here[0], there[0], sibling[1])
    for peer in group_peers[::2]:
        five_copy(peer[0], peer[0], sibling[1]).wait_recv()

    for (low_end, high_end, column), weight_norm in zip(bounds, weight_norms):
        grad = grads[:, :, column : column + high_end - low_end].reshape(
            C_MID, high_end - low_end
        )
        rate = learn_rate * (weight_norm / (jnp.sqrt(total(grad)) + norm_eps))
        fresh = momentum * velocity_flat[:, low_end:high_end] + rate * grad
        velocity_flat[:, low_end:high_end] = fresh
        next_weights[:, low_end:high_end] = params[:, low_end:high_end] - fresh
    new_velocity[...] = velocity_flat[pl.ds(gx * own_rows, own_rows), :]

    for peer, device, peer_x, peer_core in group_peers:
        velocity_copy(1, velocities.at[my_x, :, my_core], (peer, my_group), device).wait_send()
    for peer, device in y_peers:
        velocity_copy(0, velocities.at[my_x, my_y, my_core], (peer, my_y), device).wait_send()
        two_copy(peer, my_y, device).wait_send()
        four_copy(my_y, peer, device).wait_send()
    for peer, device in z_peers:
        three_copy(my_z, peer, device).wait_send()
    for peer in other_core:
        pair_copy(peer[2], peer[3]).wait_send()
    for peer, device, peer_x, peer_core in same_core:
        one_copy(peer_x, my_x, device).wait_send()
    for copy in sent_five:
        copy.wait_send()


def shards(size_x, size_y, size_z, block_input, mid_first, mid_second, out_grad, params, velocity):
    groups = size_x * CORES
    group_rows = C_MID // groups
    own_rows = group_rows // size_y
    dma = pltpu.SemaphoreType.DMA
    return pl.pallas_call(
        functools.partial(kernel, size_x, size_y, size_z),
        out_shape=(
            pltpu.VMEM((1, H_DEV, W_IMG, C_IN), BF16),
            pltpu.VMEM((own_rows, K_ROW), F32),
            pltpu.VMEM((C_MID, K_ROW), F32),
        ),
        in_specs=[pl.BlockSpec(memory_space=pl.ANY)] * 6,
        out_specs=(pl.BlockSpec(memory_space=pltpu.VMEM),) * 3,
        scratch_shapes=[
            pltpu.VMEM((H_DEV, W_IMG, C_IN), BF16),
            pltpu.VMEM((H_DEV, W_IMG * C_MID), BF16),
            pltpu.VMEM((H_DEV, W_IMG * C_MID), BF16),
            pltpu.VMEM((H_DEV, W_IMG, C_IN), BF16),
            pltpu.VMEM((C_MID, K_ROW), F32),
            pltpu.VMEM((own_rows, K_ROW), F32),
            pltpu.VMEM((PIXELS, 128), F32),
            pltpu.VMEM((PIXELS, 128), F32),
            pltpu.VMEM((PIXELS + 2 * W_PAD, 3 * C_MID), BF16),
            pltpu.VMEM((PIXELS, C_MID), BF16),
            pltpu.VMEM((C_MID, C_IN), BF16),
            pltpu.VMEM((3 * C_MID, 3 * C_MID), BF16),
            pltpu.VMEM((3 * C_MID, C_IN), BF16),
            pltpu.VMEM((C_MID, C_IN), F32),
            pltpu.VMEM((3 * C_MID, 3 * C_MID), F32),
            pltpu.VMEM((C_MID, C_IN), F32),
            pltpu.VMEM((groups, group_rows, K_PAD), F32),
            pltpu.VMEM((size_x, group_rows, K_PAD), F32),
            pltpu.VMEM((size_x, group_rows, K_PAD), F32),
            pltpu.VMEM((size_x, group_rows, K_PAD), F32),
            pltpu.VMEM((size_y, own_rows, K_PAD), F32),
            pltpu.VMEM((size_y, own_rows, K_PAD), F32),
            pltpu.VMEM((size_z, own_rows, K_PAD), F32),
            pltpu.VMEM((size_y, own_rows, K_PAD), F32),
            pltpu.VMEM((groups, group_rows, K_PAD), F32),
            pltpu.VMEM((size_x, size_y, CORES, own_rows, K_ROW), F32),
            pltpu.VMEM((C_MID, K_ROW), F32),
            dma((6,)),
            dma((size_x,)),
            dma((size_x,)),
            dma((size_x,)),
            dma((size_x,)),
            dma((size_y,)),
            dma((size_y,)),
            dma((size_z,)),
            dma((size_z,)),
            dma((size_y,)),
            dma((size_y,)),
            dma((groups,)),
            dma((groups,)),
            dma((2, max(groups, size_y))),
            dma((2, max(groups, size_y))),
        ],
        compiler_params=pltpu.CompilerParams(
            collective_id=0, has_side_effects=True, vmem_limit_bytes=62 * 1024 * 1024
        ),
        name="bottleneck_backward",
    )(block_input, mid_first, mid_second, out_grad, params, velocity)


def solution(mesh):
    return jax.shard_map(
        functools.partial(shards, ROWS_X, ROWS_Y, mesh.shape["gy"]),
        mesh=mesh,
        in_specs=(
            P(("gx", "gy"), None, None, None),
            P(("gx", "gy"), None, None),
            P(("gx", "gy"), None, None),
            P(("gx", "gy"), None, None, None),
            P(),
            P("gx", None),
        ),
        out_specs=(P(("gx", "gy"), None, None, None), P("gx", None), P()),
        check_vma=False,
    )
```
